32 devices in a mesh: gx: 4 (over y, x), gy: 8 (over z, core).
Axes of the slice: x: 2, y: 2, z: 4, core: 2. Of those that a mesh axis runs over, the one named last changes fastest.
Arguments:
- velocity_u: float32 [16, 64, 1024], P(None, 'gx', 'gy'), may hold values from -4 to 4
- velocity_v: float32 [16, 64, 1024], P(None, 'gx', 'gy'), may hold values from -4 to 4
- buoyancy: float32 [16, 64, 1024], P(None, 'gx', 'gy'), may hold values from -5 to 5
- surface: float32 [64, 1024], P('gx', 'gy'), may hold values from -0.5 to 0.5
- transport_u: float32 [64, 1024], P('gx', 'gy'), may hold values from -2 to 2
- transport_v: float32 [64, 1024], P('gx', 'gy'), may hold values from -2 to 2
- ocean: int32 [64, 1024], P('gx', 'gy'), may hold values 0 or 1
- layers: int32 [64, 1024], P('gx', 'gy'), may hold values from 4 to 16
Outputs:
- new_u: float32 [16, 64, 1024], P(None, 'gx', 'gy')
- new_v: float32 [16, 64, 1024], P(None, 'gx', 'gy')
- new_buoyancy: float32 [16, 64, 1024], P(None, 'gx', 'gy')
- new_surface: float32 [64, 1024], P('gx', 'gy')
- new_transport_u: float32 [64, 1024], P('gx', 'gy')
- new_transport_v: float32 [64, 1024], P('gx', 'gy')
The draws below stay inside these ranges and needn't reach their ends.
All inputs are finite; a program needn't handle non-finite values. No bound on the sum of `ocean` on one device may be relied on, other than what follows from the above.
Results may differ from the reference program's by a relative error of at most 0.0001.
Values sent between devices are 32-bit elements; how exact they have to be, the bound alone decides.
A program may use at most 64 MiB of HBM per device.

```python
import jax
import jax.numpy as jnp

LEVELS = 16
SUB = 8
STEPS = 2
NX = 64
NY = 1024


def plant(result, key, least, high):
    shape = result.shape
    index_at = [jax.random.randint(jax.random.fold_in(key, axis), (), 0, shape[axis]) for axis in range(len(shape))]
    result = result.at[tuple(index_at)].set(least)
    longest = shape.index(max(shape))
    index_at[longest] = (index_at[longest] + 1) % shape[longest]
    return result.at[tuple(index_at)].set(high)


def steps_of(stream_key, shape, split, least, largest):
    level, own = 1.0, jax.random.fold_in(stream_key, 6)
    for axis_at, parts in split:
        draws = jnp.exp(jax.random.uniform(jax.random.fold_in(own, axis_at), (parts,), jnp.float32, least / len(split), largest / len(split)))
        level = level * jnp.repeat(draws, shape[axis_at] // parts).reshape([-1 if axis == axis_at else 1 for axis in range(len(shape))])
    return level


def centred(own_key, shape, spread, reach, cuts=(), dtype=jnp.bfloat16):
    values = spread * jax.random.normal(own_key, shape, jnp.float32)
    if cuts:
        values = values * steps_of(own_key, shape, cuts, -0.22, 0.18)
    return jnp.clip(values, -reach, reach).astype(dtype)


def setup_inputs(seed: int = 0) -> dict:
    arg_keys = jax.random.split(jax.random.key(seed), 9)
    velocity_u = centred(arg_keys[0], (LEVELS, NX, NY), 0.5, 4.0, ((1, 4), (2, 8)), jnp.float32)
    velocity_v = centred(arg_keys[1], (LEVELS, NX, NY), 0.5, 4.0, ((1, 4), (2, 8)), jnp.float32)
    buoyancy = centred(arg_keys[2], (LEVELS, NX, NY), 1.0, 5.0, ((1, 4), (2, 8)), jnp.float32)
    surface = centred(arg_keys[3], (NX, NY), 0.1, 0.5, ((0, 4), (1, 8)), jnp.float32)
    transport_u = centred(arg_keys[4], (NX, NY), 0.3, 2.0, ((0, 4), (1, 8)), jnp.float32)
    transport_v = centred(arg_keys[5], (NX, NY), 0.3, 2.0, ((0, 4), (1, 8)), jnp.float32)
    ocean = plant((jax.random.randint(arg_keys[6], (NX, NY), 0, 8) < 7).astype(jnp.int32), jax.random.fold_in(arg_keys[6], 1), 0, 1)
    layers = plant(jax.random.randint(arg_keys[7], (NX, NY), LEVELS // 4, LEVELS + 1), jax.random.fold_in(arg_keys[7], 1), LEVELS // 4, LEVELS).astype(jnp.int32)
    return dict(velocity_u=velocity_u, velocity_v=velocity_v, buoyancy=buoyancy, surface=surface, transport_u=transport_u, transport_v=transport_v, ocean=ocean, layers=layers)


PRESSURE_COEF = 0.5
CORIOLIS = 0.1
VISCOSITY = 0.02
TIME_STEP = 0.2
DIVERGENCE_COEF = 0.25
GRAVITY_COEF = 0.25
DRAG_KEEP = 0.98
SURFACE_CORIOLIS = 0.05


def trim_rim(field, width):
    return field[..., width:field.shape[-2] - width, width:field.shape[-1] - width]


def diff_x(field):
    return (field[..., 2:, 1:-1] - field[..., :-2, 1:-1]) * 0.5


def diff_y(field):
    return (field[..., 1:-1, 2:] - field[..., 1:-1, :-2]) * 0.5


def laplace(field):
    return (field[..., 2:, 1:-1] + field[..., :-2, 1:-1] + field[..., 1:-1, 2:]
            + field[..., 1:-1, :-2] - 4.0 * field[..., 1:-1, 1:-1])


def pad_rim(field, width):
    spec = [(0, 0)] * (field.ndim - 2) + [(width, width), (width, width)]
    return jnp.pad(field, spec)


def advance(near_state, biharm, active):
    levels = near_state.shape[1]
    vel_u = trim_rim(near_state[0], 1)
    vel_v = trim_rim(near_state[1], 1)
    buoy_near = near_state[2]
    pressure = jnp.cumsum(buoy_near, axis=0) / levels
    tend_u = -PRESSURE_COEF * diff_x(pressure) + CORIOLIS * vel_v - VISCOSITY * biharm[0]
    tend_v = -PRESSURE_COEF * diff_y(pressure) - CORIOLIS * vel_u - VISCOSITY * biharm[1]
    tend_b = -(vel_u * diff_x(buoy_near) + vel_v * diff_y(buoy_near)) - VISCOSITY * biharm[2]
    star_u = active * (vel_u + TIME_STEP * tend_u)
    star_v = active * (vel_v + TIME_STEP * tend_v)
    new_buoy = active * (trim_rim(buoy_near, 1) + TIME_STEP * tend_b)
    force_u = jnp.sum(active * tend_u, axis=0) / levels
    force_v = jnp.sum(active * tend_v, axis=0) / levels
    return star_u, star_v, new_buoy, force_u, force_v


def surface_step(sea_level, flow_u, flow_v, force_u, force_v, wet_mask, column_depth):
    eta_mid = trim_rim(wet_mask, 1) * (trim_rim(sea_level, 1)
                                       - DIVERGENCE_COEF * (diff_x(flow_u) + diff_y(flow_v)))
    wet_inner = trim_rim(wet_mask, 2)
    total_depth = trim_rim(column_depth, 2) + trim_rim(eta_mid, 1)
    old_u = trim_rim(flow_u, 2)
    old_v = trim_rim(flow_v, 2)
    next_u = wet_inner * (DRAG_KEEP * old_u + TIME_STEP * trim_rim(force_u, 2)
                          - GRAVITY_COEF * total_depth * diff_x(eta_mid) + SURFACE_CORIOLIS * old_v)
    next_v = wet_inner * (DRAG_KEEP * old_v + TIME_STEP * trim_rim(force_v, 2)
                          - GRAVITY_COEF * total_depth * diff_y(eta_mid) - SURFACE_CORIOLIS * old_u)
    return (trim_rim(eta_mid, 1), next_u, next_v, trim_rim(force_u, 2), trim_rim(force_v, 2),
            wet_inner, trim_rim(column_depth, 2))


def couple_columns(star_u, star_v, total_u, total_v, active, layer_count, column_depth, substeps):
    column_u = jnp.sum(star_u, axis=0) / layer_count
    column_v = jnp.sum(star_v, axis=0) / layer_count
    new_u = active * (star_u - column_u + (total_u / substeps) / column_depth)
    new_v = active * (star_v - column_v + (total_v / substeps) / column_depth)
    return new_u, new_v


def reference(velocity_u, velocity_v, buoyancy, surface, transport_u, transport_v, ocean, layers):
    levels = velocity_u.shape[0]
    wet_mask = ocean.astype(jnp.float32)
    active = wet_mask[None] * (jnp.arange(levels)[:, None, None] < layers[None]).astype(jnp.float32)
    layer_count = layers.astype(jnp.float32)
    column_depth = layer_count / levels
    stacked = jnp.stack([velocity_u, velocity_v, buoyancy])
    sea_level, flow_u, flow_v = surface, transport_u, transport_v
    for step_index in range(STEPS):
        near_state = pad_rim(stacked, 1)
        lap_masked = active * laplace(near_state)
        biharm = laplace(pad_rim(lap_masked, 1))
        star_u, star_v, new_buoy, force_u, force_v = advance(near_state, biharm, active)
        total_u = jnp.zeros(surface.shape, jnp.float32)
        total_v = jnp.zeros(surface.shape, jnp.float32)
        for sub_index in range(SUB):
            pieces = surface_step(*[pad_rim(item, 2) for item in
                                    (sea_level, flow_u, flow_v, force_u, force_v, wet_mask, column_depth)])
            sea_level, flow_u, flow_v = pieces[0], pieces[1], pieces[2]
            total_u = total_u + flow_u
            total_v = total_v + flow_v
        new_u, new_v = couple_columns(star_u, star_v, total_u, total_v, active, layer_count,
                                      column_depth, SUB)
        stacked = jnp.stack([new_u, new_v, new_buoy])
    return (stacked[0], stacked[1], stacked[2], sea_level, flow_u, flow_v)
```

```python
import jax
import jax.numpy as jnp
from jax import lax
from jax.experimental import pallas as pl
from jax.experimental.pallas import tpu as pltpu
from jax.sharding import PartitionSpec as P

SUB = 8
STEPS = 2
LANES = 128
ROWS = 16
LEVELS = 16
FIELDS = 3
STACK = FIELDS * LEVELS
MESH = pl.DeviceIdType.MESH
F32 = jnp.float32

DIRS = [(-1, 0), (1, 0), (0, -1), (0, 1), (-1, -1), (-1, 1), (1, -1), (1, 1)]
SIDES = [(-1, -1), (0, -1), (1, -1), (-1, 1), (0, 1), (1, 1)]
FAR = STACK
FLAT = 2 * STACK


def turn(x, shift, axis):
    return pltpu.roll(x, shift % x.shape[axis] if isinstance(shift, int) else shift, axis)


def kernel(
    vel_u, vel_v, buoy, surface, trans_u, trans_v, ocean, layers,
    out_u, out_v, out_b, out_eta, out_tu, out_tv,
    fx, lp, dyb, star_u, star_v, near_ext, code_ext,
    x_send, y_send, x_recv, y_recv, fx_send, fy_send, fx_recv, fy_recv,
    send_sem, recv_sem,
):
    gx, gy = lax.axis_index("gx"), lax.axis_index("gy")
    nx, ny = lax.axis_size("gx"), lax.axis_size("gy")

    def exists(d):
        ok = jnp.bool_(True)
        if d[0] == -1:
            ok = jnp.logical_and(ok, gx > 0)
        if d[0] == 1:
            ok = jnp.logical_and(ok, gx < nx - 1)
        if d[1] == -1:
            ok = jnp.logical_and(ok, gy > 0)
        if d[1] == 1:
            ok = jnp.logical_and(ok, gy < ny - 1)
        return ok

    here = {d: exists(d) for d in DIRS}
    barrier = pltpu.get_barrier_semaphore()
    total_near = jnp.int32(0)
    for d in DIRS:
        total_near = total_near + here[d].astype(jnp.int32)

        @pl.when(here[d])
        def _(d=d):
            pl.semaphore_signal(barrier, inc=1, device_id=(gx + d[0], gy + d[1]), device_id_type=MESH)

    for d in DIRS:
        @pl.when(jnp.logical_not(here[d]))
        def _(d=d):
            for p in range(STEPS):
                if d[1] == 0:
                    s = 0 if d[0] < 0 else 1
                    x_recv[p, s] = jnp.zeros(x_recv.shape[2:], F32)
                    fx_recv[p, s] = jnp.zeros(fx_recv.shape[2:], F32)
                else:
                    s = SIDES.index(d)
                    y_recv[p, s] = jnp.zeros(y_recv.shape[2:], F32)
                    fy_recv[p, s] = jnp.zeros(fy_recv.shape[2:], F32)

    def copies(phase, step):
        result = []
        for i, d in enumerate(DIRS):
            back = (-d[0], -d[1])
            if d[1] == 0:
                src_at, dst_at = (0 if d[0] < 0 else 1), (0 if back[0] < 0 else 1)
                if phase == 0:
                    src, dst = x_send.at[step, src_at], x_recv.at[step, dst_at]
                    if step:
                        short = FLAT + 3 * ROWS
                        src, dst = src.at[pl.ds(0, short)], dst.at[pl.ds(0, short)]
                else:
                    src, dst = fx_send.at[step], fx_recv.at[step, dst_at]
            else:
                src_at, dst_at = (0 if d[1] < 0 else 1), SIDES.index(back)
                if phase == 0:
                    src, dst = y_send.at[step, src_at], y_recv.at[step, dst_at]
                else:
                    src, dst = fy_send.at[step, src_at], fy_recv.at[step, dst_at]
            at = phase * STEPS + step
            copy = pltpu.make_async_remote_copy(
                src_ref=src, dst_ref=dst,
                send_sem=send_sem.at[at, i], recv_sem=recv_sem.at[at, DIRS.index(back)],
                device_id=(gx + d[0], gy + d[1]), device_id_type=MESH,
            )
            result.append((d, copy))
        return result

    def start(phase, step):
        for d, copy in copies(phase, step):
            @pl.when(here[d])
            def _(copy=copy):
                copy.start()

    def arrive(phase, step):
        by_dir = dict(copies(phase, step))
        for d in DIRS:
            @pl.when(here[d])
            def _(d=d):
                by_dir[(-d[0], -d[1])].wait_recv()

    def sent(phase, step):
        for d, copy in copies(phase, step):
            @pl.when(here[d])
            def _(copy=copy):
                copy.wait_send()

    lane = lax.broadcasted_iota(jnp.int32, (ROWS, LANES), 1)
    pair = lane >> 1
    odd = (lane & 1) == 1
    zero = jnp.zeros((ROWS, LANES), F32)

    def put(step, j, cells, strips):
        fx[j, pl.ds(2, ROWS)] = cells
        x_send[step, 0, pl.ds(j, 1)] = cells[0:1]
        x_send[step, 0, pl.ds(FAR + j, 1)] = cells[1:2]
        x_send[step, 1, pl.ds(j, 1)] = cells[ROWS - 1 : ROWS]
        x_send[step, 1, pl.ds(FAR + j, 1)] = cells[ROWS - 2 : ROWS - 1]
        to_left, to_right = strips
        rolled = pltpu.roll(cells, 2 * j + 2, 1)
        to_right = jnp.where(pair == j, rolled, to_right)
        to_left = jnp.where(pair == j + 1, rolled, to_left)
        return to_left, to_right

    def pack_flat(arrays):
        to_left, to_right = zero, zero
        for a, cells in enumerate(arrays):
            rolled = turn(cells, 16 * a + 16, 1)
            to_right = jnp.where((lane >> 4) == a, rolled, to_right)
            to_left = jnp.where((lane >> 4) == a + 1, rolled, to_left)
        return to_left, to_right

    def send_state(step, strips, flats):
        y_send[step, 0, 0:ROWS] = strips[0]
        y_send[step, 1, 0:ROWS] = strips[1]
        flat_left, flat_right = pack_flat(flats)
        y_send[step, 0, ROWS : 2 * ROWS] = flat_left
        y_send[step, 1, ROWS : 2 * ROWS] = flat_right
        for s in range(2):
            for a, cells in enumerate(flats):
                x_send[step, s, FLAT + ROWS * a : FLAT + ROWS * (a + 1)] = cells
        start(0, step)

    def side_of(from_left, from_right, a):
        cells = jnp.where(
            (lane >> 4) == a + 1, from_right, jnp.where((lane >> 4) == a, from_left, 0.0)
        )
        return turn(cells, -(16 * a + 16), 1)

    def wide(own, up, down, sides, a):
        main = jnp.concatenate([up, own, down], axis=0)
        side = jnp.concatenate([side_of(sides[r], sides[r + 3], a) for r in range(3)], axis=0)
        return jnp.concatenate([main, side], axis=1)

    lay = layers[...].astype(F32)
    code = jnp.where(ocean[...] > 0, lay, 0.0)

    strips = (zero, zero)
    for a, ref in enumerate((vel_u, vel_v, buoy)):
        def pack(k, strips, a=a, ref=ref):
            return put(0, a * LEVELS + k, ref[k], strips)

        strips = lax.fori_loop(0, LEVELS, pack, strips, unroll=True)
    pl.semaphore_wait(barrier, total_near)
    sea, flow_u, flow_v = surface[...], trans_u[...], trans_v[...]
    send_state(0, strips, (sea, flow_u, flow_v, code))

    lane18 = lax.broadcasted_iota(jnp.int32, (ROWS + 2, LANES), 1)
    for step in range(STEPS):
        arrive(0, step)
        from_left, from_right = y_recv[step, 1, 0:ROWS], y_recv[step, 4, 0:ROWS]
        near = jnp.where(odd, from_left, turn(from_right, -2, 1))
        far = jnp.where(odd, turn(from_left, 1, 1), turn(from_right, -3, 1))
        inner = turn(jnp.where(odd, strips[1], strips[0]), -1, 1)
        near_ext[pl.ds(1, ROWS)] = near
        odd8 = odd[0:8]
        top = jnp.where(odd8, y_recv[step, 0, 8:16], turn(y_recv[step, 3, 8:16], -2, 1))
        low = jnp.where(odd8, y_recv[step, 2, 0:8], turn(y_recv[step, 5, 0:8], -2, 1))
        near_ext[pl.ds(0, 1)] = top[7:8]
        near_ext[pl.ds(ROWS + 1, 1)] = low[0:1]

        flats_y = [y_recv[step, r, ROWS : 2 * ROWS] for r in range(6)]

        def flat_x(s, a):
            return x_recv[step, s, FLAT + ROWS * a : FLAT + ROWS * (a + 1)]

        if step == 0:
            code_wide = wide(code, flat_x(0, 3), flat_x(1, 3), flats_y, 3)
            code_ext[...] = code_wide[:, 0:LANES]
            code_side = code_wide[ROWS : 2 * ROWS, LANES:]
            code_near = jnp.where(
                odd,
                jnp.broadcast_to(code_side[:, LANES - 1 : LANES], (ROWS, LANES)),
                jnp.broadcast_to(code_side[:, 0:1], (ROWS, LANES)),
            )
            act_near = ((pair & (LEVELS - 1)).astype(F32) < code_near).astype(F32)
        lap_near = act_near * (
            far + inner + near_ext[pl.ds(0, ROWS)] + near_ext[pl.ds(2, ROWS)] - 4.0 * near
        )
        near18 = near_ext[pl.ds(0, ROWS + 2)]
        code18 = code_ext[pl.ds(ROWS - 1, ROWS + 2)]

        def biharm(j, act18, keep):
            fx[j, pl.ds(0, 1)] = x_recv[step, 0, pl.ds(FAR + j, 1)]
            fx[j, pl.ds(1, 1)] = x_recv[step, 0, pl.ds(j, 1)]
            fx[j, pl.ds(ROWS + 2, 1)] = x_recv[step, 1, pl.ds(j, 1)]
            fx[j, pl.ds(ROWS + 3, 1)] = x_recv[step, 1, pl.ds(FAR + j, 1)]
            mid = fx[j, pl.ds(1, ROWS + 2)]
            edge = pltpu.roll(near18, 127 - 2 * j, 1)
            ahead = jnp.where(lane18 == LANES - 1, edge, turn(mid, -1, 1))
            behind = jnp.where(lane18 == 0, edge, turn(mid, 1, 1))
            lap = act18 * (
                fx[j, pl.ds(0, ROWS + 2)] + fx[j, pl.ds(2, ROWS + 2)] + ahead + behind - 4.0 * mid
            )
            lp[j, pl.ds(0, ROWS + 2)] = lap
            if keep is not None:
                dyb[keep, pl.ds(0, ROWS + 2)] = ahead - behind
            mid = lp[j, pl.ds(1, ROWS)]
            edge = pltpu.roll(lap_near, 127 - 2 * j, 1)
            ahead = jnp.where(lane == LANES - 1, edge, turn(mid, -1, 1))
            behind = jnp.where(lane == 0, edge, turn(mid, 1, 1))
            return lp[j, pl.ds(0, ROWS)] + lp[j, pl.ds(2, ROWS)] + ahead + behind - 4.0 * mid

        def level(k, carry):
            press_x, press_y, force_u, force_v, col_u, col_v = carry
            level_at = lax.convert_element_type(k, F32)
            act18 = (level_at < code18).astype(F32)
            act = (level_at < code).astype(F32)
            bih_u = biharm(k, act18, None)
            bih_v = biharm(LEVELS + k, act18, None)
            bih_b = biharm(2 * LEVELS + k, act18, k)
            u, v = fx[k, pl.ds(2, ROWS)], fx[LEVELS + k, pl.ds(2, ROWS)]
            at = 2 * LEVELS + k
            b = fx[at, pl.ds(2, ROWS)]
            b_x = fx[at, pl.ds(3, ROWS)] - fx[at, pl.ds(1, ROWS)]
            b_y = dyb[k, pl.ds(1, ROWS)]
            press_x, press_y = press_x + b_x, press_y + b_y
            tend_u = (-0.25 / LEVELS) * press_x + 0.1 * v - 0.02 * bih_u
            tend_v = (-0.25 / LEVELS) * press_y - 0.1 * u - 0.02 * bih_v
            tend_b = -0.5 * (u * b_x + v * b_y) - 0.02 * bih_b
            su = act * (u + 0.2 * tend_u)
            sv = act * (v + 0.2 * tend_v)
            star_u[k] = su
            star_v[k] = sv
            new_b = act * (b + 0.2 * tend_b)
            if step == STEPS - 1:
                out_b[k] = new_b
            else:
                fx[at, pl.ds(2, ROWS)] = new_b
            return (
                press_x, press_y, force_u + act * tend_u, force_v + act * tend_v,
                col_u + su, col_v + sv,
            )

        _, _, force_u, force_v, col_u, col_v = lax.fori_loop(
            0, LEVELS, level, (zero,) * 6, unroll=True
        )
        force_u, force_v = force_u / LEVELS, force_v / LEVELS
        fx_send[step, 0:ROWS] = force_u
        fx_send[step, ROWS : 2 * ROWS] = force_v
        flat_left, flat_right = pack_flat((force_u, force_v))
        fy_send[step, 0] = flat_left
        fy_send[step, 1] = flat_right
        start(1, step)

        wet = (code_wide > 0.0).astype(F32)
        depth = code_wide / LEVELS
        state = tuple(
            wide(own, flat_x(0, a), flat_x(1, a), flats_y, a)
            for a, own in enumerate((sea, flow_u, flow_v))
        )
        if step < STEPS - 1:
            def pack_b(k, strips):
                j = 2 * LEVELS + k
                return put(step + 1, j, fx[j, pl.ds(2, ROWS)], strips)

            strips = lax.fori_loop(0, LEVELS, pack_b, (zero, zero), unroll=True)
        arrive(1, step)
        sides = [fy_recv[step, r] for r in range(6)]
        push_u, push_v = (
            0.2 * wide(
                own, fx_recv[step, 0, ROWS * a : ROWS * (a + 1)],
                fx_recv[step, 1, ROWS * a : ROWS * (a + 1)], sides, a,
            )
            for a, own in enumerate((force_u, force_v))
        )

        def substep(_, carry):
            eta, tu, tv, sum_u, sum_v = carry
            div = (turn(tu, -1, 0) - turn(tu, 1, 0)) + (turn(tv, -1, 1) - turn(tv, 1, 1))
            eta = wet * (eta - 0.125 * div)
            thick = 0.125 * (depth + eta)
            new_u = wet * (
                0.98 * tu + push_u - thick * (turn(eta, -1, 0) - turn(eta, 1, 0)) + 0.05 * tv
            )
            new_v = wet * (
                0.98 * tv + push_v - thick * (turn(eta, -1, 1) - turn(eta, 1, 1)) - 0.05 * tu
            )
            sum_u = sum_u + new_u[ROWS : 2 * ROWS, 0:LANES]
            sum_v = sum_v + new_v[ROWS : 2 * ROWS, 0:LANES]
            return eta, new_u, new_v, sum_u, sum_v

        eta, tu, tv, sum_u, sum_v = lax.fori_loop(0, SUB, substep, state + (zero, zero))
        sea, flow_u, flow_v = (c[ROWS : 2 * ROWS, 0:LANES] for c in (eta, tu, tv))
        scale = LEVELS / SUB
        shift_u = (scale * sum_u - col_u) / lay
        shift_v = (scale * sum_v - col_v) / lay

        if step == STEPS - 1:
            def finish(k, carry):
                act = (lax.convert_element_type(k, F32) < code).astype(F32)
                out_u[k] = act * (star_u[k] + shift_u)
                out_v[k] = act * (star_v[k] + shift_v)
                return carry

            lax.fori_loop(0, LEVELS, finish, 0, unroll=True)
            out_eta[...] = sea
            out_tu[...] = flow_u
            out_tv[...] = flow_v
        else:
            def couple(k, strips):
                act = (lax.convert_element_type(k, F32) < code).astype(F32)
                strips = put(step + 1, k, act * (star_u[k] + shift_u), strips)
                return put(step + 1, LEVELS + k, act * (star_v[k] + shift_v), strips)

            strips = lax.fori_loop(0, LEVELS, couple, strips, unroll=True)
            send_state(step + 1, strips, (sea, flow_u, flow_v))

    for step in range(STEPS):
        sent(0, step)
        sent(1, step)


def per_device(velocity_u, velocity_v, buoyancy, surface, transport_u, transport_v, ocean, layers):
    cube = jax.ShapeDtypeStruct(velocity_u.shape, F32)
    flat = jax.ShapeDtypeStruct(surface.shape, F32)
    vmem = pl.BlockSpec(memory_space=pltpu.VMEM)
    ext = 24
    return tuple(
        pl.pallas_call(
            kernel,
            out_shape=(cube, cube, cube, flat, flat, flat),
            in_specs=[vmem] * 8,
            out_specs=(vmem,) * 6,
            scratch_shapes=[
                pltpu.VMEM((STACK, ext, LANES), F32),
                pltpu.VMEM((STACK, ext, LANES), F32),
                pltpu.VMEM((LEVELS, ext, LANES), F32),
                pltpu.VMEM((LEVELS, ROWS, LANES), F32),
                pltpu.VMEM((LEVELS, ROWS, LANES), F32),
                pltpu.VMEM((ext, LANES), F32),
                pltpu.VMEM((3 * ROWS, LANES), F32),
                pltpu.VMEM((STEPS, 2, FLAT + 4 * ROWS, LANES), F32),
                pltpu.VMEM((STEPS, 2, 2 * ROWS, LANES), F32),
                pltpu.VMEM((STEPS, 2, FLAT + 4 * ROWS, LANES), F32),
                pltpu.VMEM((STEPS, 6, 2 * ROWS, LANES), F32),
                pltpu.VMEM((STEPS, 2 * ROWS, LANES), F32),
                pltpu.VMEM((STEPS, 2, ROWS, LANES), F32),
                pltpu.VMEM((STEPS, 2, 2 * ROWS, LANES), F32),
                pltpu.VMEM((STEPS, 6, ROWS, LANES), F32),
                pltpu.SemaphoreType.DMA((2 * STEPS, 8)),
                pltpu.SemaphoreType.DMA((2 * STEPS, 8)),
            ],
            compiler_params=pltpu.CompilerParams(
                collective_id=0, has_side_effects=True, vmem_limit_bytes=24 * 2**20
            ),
        )(velocity_u, velocity_v, buoyancy, surface, transport_u, transport_v, ocean, layers)
    )


def solution(mesh):
    cube, flat = P(None, "gx", "gy"), P("gx", "gy")
    return jax.shard_map(
        per_device,
        mesh=mesh,
        in_specs=(cube, cube, cube, flat, flat, flat, flat, flat),
        out_specs=(cube, cube, cube, flat, flat, flat),
        check_vma=False,
    )
```

```python
import jax
import jax.numpy as jnp
from jax import lax
from jax.experimental import pallas as pl
from jax.experimental.pallas import tpu as pltpu
from jax.sharding import PartitionSpec as P

SUB = 8
STEPS = 2
LANES = 128
ROWS = 16
LEVELS = 16
FIELDS = 3
STACK = FIELDS * LEVELS
MESH = pl.DeviceIdType.MESH
F32 = jnp.float32

DIRS = [(-1, 0), (1, 0), (0, -1), (0, 1), (-1, -1), (-1, 1), (1, -1), (1, 1)]
SIDES = [(-1, -1), (0, -1), (1, -1), (-1, 1), (0, 1), (1, 1)]
MOVING = 2 * LEVELS
CODE_ROW = 2 * STACK
RIM = CODE_ROW + 8
HALF = LANES // 2


RIMS, FORCE, PLANE, EARLY = 0, 1, 2, 3


def turn(x, shift, axis):
    return pltpu.roll(x, shift % x.shape[axis] if isinstance(shift, int) else shift, axis)


def fold(cells):
    low = lax.broadcasted_iota(jnp.int32, (8, LANES), 1) < HALF
    return jnp.where(low, cells[0:8], turn(cells[8:16], HALF, 1))


def unfold(cells):
    return jnp.concatenate([cells, turn(cells, HALF, 1)], axis=0)


def pack_flat(arrays):
    lane = lax.broadcasted_iota(jnp.int32, (ROWS, LANES), 1)
    to_left = to_right = jnp.zeros((ROWS, LANES), F32)
    for a, cells in enumerate(arrays):
        to_right = jnp.where((lane >> 4) == a, turn(cells, 16 * a + 16, 1), to_right)
        to_left = jnp.where((lane >> 4) == a, turn(cells, 16 * a, 1), to_left)
    return fold(to_left), fold(to_right)


def wide(own, up, down, sides, a):
    lane = lax.broadcasted_iota(jnp.int32, (ROWS, LANES), 1)
    blocks = []
    for r in range(3):
        from_left, from_right = unfold(sides[r]), unfold(sides[r + 3])
        left, right = turn(from_left, 112 - 16 * a, 1), turn(from_right, -16 * a, 1)
        blocks.append(jnp.where(lane < 16, right, jnp.where(lane >= 112, left, 0.0)))
    main = jnp.concatenate([up, own, down], axis=0)
    return jnp.concatenate([main, jnp.concatenate(blocks, axis=0)], axis=1)


def barotropic(state, push_u, push_v, code_wide):
    wet = (code_wide > 0.0).astype(F32)
    depth = code_wide / LEVELS
    zero = jnp.zeros((ROWS, LANES), F32)

    def substep(_, carry):
        eta, tu, tv, sum_u, sum_v = carry
        div = (turn(tu, -1, 0) - turn(tu, 1, 0)) + (turn(tv, -1, 1) - turn(tv, 1, 1))
        eta = wet * (eta - 0.125 * div)
        thick = 0.125 * (depth + eta)
        new_u = wet * (
            0.98 * tu + push_u - thick * (turn(eta, -1, 0) - turn(eta, 1, 0)) + 0.05 * tv
        )
        new_v = wet * (
            0.98 * tv + push_v - thick * (turn(eta, -1, 1) - turn(eta, 1, 1)) - 0.05 * tu
        )
        sum_u = sum_u + new_u[ROWS : 2 * ROWS, 0:LANES]
        sum_v = sum_v + new_v[ROWS : 2 * ROWS, 0:LANES]
        return eta, new_u, new_v, sum_u, sum_v

    eta, tu, tv, sum_u, sum_v = lax.fori_loop(0, SUB, substep, state + (zero, zero))
    own = tuple(c[ROWS : 2 * ROWS, 0:LANES] for c in (eta, tu, tv))
    return own, sum_u, sum_v


def finish_kernel(
    hbm_u, hbm_v, new_b, hbm_columns, hbm_wide,
    out_u, out_v, out_b, out_eta, out_tu, out_tv,
    star_u, star_v, columns, wide_in, buf_u, buf_v, buf_flat, sem, in_sem,
):
    loads = [
        pltpu.make_async_copy(src, dst, in_sem.at[i])
        for i, (src, dst) in enumerate((
            (hbm_wide, wide_in), (hbm_columns, columns), (hbm_u, star_u), (hbm_v, star_v)
        ))
    ]
    for load in loads:
        load.start()
    copies = [pltpu.make_async_copy(new_b, out_b, sem.at[0])]
    copies[0].start()
    loads[0].wait()
    code_wide = wide_in[3]
    own, sum_u, sum_v = barotropic(
        (wide_in[0], wide_in[1], wide_in[2]), wide_in[4], wide_in[5], code_wide
    )
    for a, (cells, out) in enumerate(zip(own, (out_eta, out_tu, out_tv))):
        buf_flat[a] = cells
        copies.append(pltpu.make_async_copy(buf_flat.at[a], out, sem.at[1 + a]))
        copies[-1].start()
    code = code_wide[ROWS : 2 * ROWS, 0:LANES]
    lay = jnp.maximum(code, 1.0)
    scale = LEVELS / SUB
    for load in loads[1:]:
        load.wait()
    for a, (star, buf, out, total) in enumerate(
        ((star_u, buf_u, out_u, sum_u), (star_v, buf_v, out_v, sum_v))
    ):
        shift = (scale * total - columns[a]) / lay

        def finish(k, carry, star=star, buf=buf, shift=shift):
            act = lax.convert_element_type(k, F32) < code
            buf[k] = jnp.where(act, star[k] + shift, 0.0)
            return carry

        lax.fori_loop(0, LEVELS, finish, 0, unroll=True)
        copies.append(pltpu.make_async_copy(buf, out, sem.at[4 + a]))
        copies[-1].start()
    for copy in copies:
        copy.wait()


def kernel(
    vel_u, vel_v, buoy, surface, trans_u, trans_v, ocean, layers,
    hbm_u, hbm_v, hbm_b, hbm_columns, hbm_wide,
    star_u, star_v, out_b, out_columns, out_wide, out_sem,
    fx, lp, dyb, near_ext, code_ext, in_3d, in_2d, in_int,
    x_send, y_send, x_recv, y_recv, gx_send, gy_send, gx_recv, gy_recv,
    fx_send, fy_send, fx_recv, fy_recv, in_sem, send_sem, recv_sem,
):
    loads = []
    for a, ref in enumerate((vel_u, vel_v, buoy)):
        loads.append(pltpu.make_async_copy(ref, in_3d.at[a], in_sem.at[a]))
    for a, ref in enumerate((surface, trans_u, trans_v)):
        loads.append(pltpu.make_async_copy(ref, in_2d.at[a], in_sem.at[3 + a]))
    for a, ref in enumerate((ocean, layers)):
        loads.append(pltpu.make_async_copy(ref, in_int.at[a], in_sem.at[6 + a]))
    for load in loads:
        load.start()
    gx, gy = lax.axis_index("gx"), lax.axis_index("gy")
    nx, ny = lax.axis_size("gx"), lax.axis_size("gy")

    def exists(d):
        ok = jnp.bool_(True)
        if d[0] == -1:
            ok = jnp.logical_and(ok, gx > 0)
        if d[0] == 1:
            ok = jnp.logical_and(ok, gx < nx - 1)
        if d[1] == -1:
            ok = jnp.logical_and(ok, gy > 0)
        if d[1] == 1:
            ok = jnp.logical_and(ok, gy < ny - 1)
        return ok

    here = {d: exists(d) for d in DIRS}
    barrier = pltpu.get_barrier_semaphore()
    total_near = jnp.int32(0)
    for d in DIRS:
        total_near = total_near + here[d].astype(jnp.int32)

        @pl.when(here[d])
        def _(d=d):
            pl.semaphore_signal(barrier, inc=1, device_id=(gx + d[0], gy + d[1]), device_id_type=MESH)

    for d in DIRS:
        @pl.when(jnp.logical_not(here[d]))
        def _(d=d):
            for p in range(STEPS):
                if d[1] == 0:
                    s = 0 if d[0] < 0 else 1
                    x_recv[p, s] = jnp.zeros(x_recv.shape[2:], F32)
                    gx_recv[p, s] = jnp.zeros(gx_recv.shape[2:], F32)
                    fx_recv[p, s] = jnp.zeros(fx_recv.shape[2:], F32)
                else:
                    s = SIDES.index(d)
                    y_recv[p, s] = jnp.zeros(y_recv.shape[2:], F32)
                    gy_recv[p, s] = jnp.zeros(gy_recv.shape[2:], F32)
                    fy_recv[p, s] = jnp.zeros(fy_recv.shape[2:], F32)

    def copies(phase, step):
        result = []
        for i, d in enumerate(DIRS):
            back = (-d[0], -d[1])
            if d[1] == 0:
                src_at, dst_at = (0 if d[0] < 0 else 1), (0 if back[0] < 0 else 1)
                if phase == FORCE:
                    src, dst = fx_send.at[step], fx_recv.at[step, dst_at]
                elif phase == PLANE:
                    rows = pl.ds(0, (4 if step == 0 else 3) * ROWS)
                    src, dst = gx_send.at[step, rows], gx_recv.at[step, dst_at, rows]
                else:
                    if step == 0:
                        rows = pl.ds(0, RIM)
                    elif phase == EARLY:
                        rows = pl.ds(2 * MOVING, 2 * LEVELS)
                    else:
                        rows = pl.ds(0, 2 * MOVING)
                    src, dst = x_send.at[step, src_at, rows], x_recv.at[step, dst_at, rows]
            else:
                src_at, dst_at = (0 if d[1] < 0 else 1), SIDES.index(back)
                if phase == FORCE:
                    src, dst = fy_send.at[step, src_at], fy_recv.at[step, dst_at]
                elif phase == PLANE:
                    src, dst = gy_send.at[step, src_at], gy_recv.at[step, dst_at]
                elif phase == EARLY:
                    continue
                else:
                    src, dst = y_send.at[step, src_at], y_recv.at[step, dst_at]
                    if d[0] != 0:
                        rows = pl.ds(0, 8) if d[0] < 0 else pl.ds(8, 8)
                        src, dst = src.at[rows], dst.at[rows]
            at = phase * STEPS + step
            copy = pltpu.make_async_remote_copy(
                src_ref=src, dst_ref=dst,
                send_sem=send_sem.at[at, i], recv_sem=recv_sem.at[at, DIRS.index(back)],
                device_id=(gx + d[0], gy + d[1]), device_id_type=MESH,
            )
            result.append((d, copy))
        return result

    def start(phase, step):
        for d, copy in copies(phase, step):
            @pl.when(here[d])
            def _(copy=copy):
                copy.start()

    def arrive(phase, step):
        by_dir = dict(copies(phase, step))
        for d in by_dir:
            @pl.when(here[d])
            def _(d=d):
                by_dir[(-d[0], -d[1])].wait_recv()

    def sent(phase, step):
        for d, copy in copies(phase, step):
            @pl.when(here[d])
            def _(copy=copy):
                copy.wait_send()

    lane = lax.broadcasted_iota(jnp.int32, (ROWS, LANES), 1)
    pair = lane >> 1
    odd = (lane & 1) == 1
    zero = jnp.zeros((ROWS, LANES), F32)

    def put(step, j, near_at, far_at, cells, strips):
        x_send[step, 0, pl.ds(near_at, 1)] = cells[0:1]
        x_send[step, 0, pl.ds(far_at, 1)] = cells[1:2]
        x_send[step, 1, pl.ds(near_at, 1)] = cells[ROWS - 1 : ROWS]
        x_send[step, 1, pl.ds(far_at, 1)] = cells[ROWS - 2 : ROWS - 1]
        to_left, to_right = strips
        rolled = turn(cells, 2 * j + 2, 1)
        to_right = jnp.where(pair == j, rolled, to_right)
        to_left = jnp.where(pair == j + 1, rolled, to_left)
        return to_left, to_right

    def put_v(step, j, cells, strips):
        fx[j, pl.ds(2, ROWS)] = cells
        return put(step, j, j, MOVING + j, cells, strips)

    def put_b(step, k, cells, strips):
        j = MOVING + k
        return put(step, j, 2 * MOVING + k, 2 * MOVING + LEVELS + k, cells, strips)

    def send_state(step, strips, flats):
        y_send[step, 0] = strips[0]
        y_send[step, 1] = strips[1]
        start(RIMS, step)
        flat_left, flat_right = pack_flat(flats)
        gy_send[step, 0] = flat_left
        gy_send[step, 1] = flat_right
        for a, cells in enumerate(flats):
            gx_send[step, ROWS * a : ROWS * (a + 1)] = cells
        start(PLANE, step)

    loads[6].wait()
    loads[7].wait()
    lay = in_int[1].astype(F32)
    code = jnp.where(in_int[0] > 0, lay, 0.0)
    strips = put(0, STACK, CODE_ROW, CODE_ROW + 1, code, (zero, zero))
    for a in range(FIELDS):
        loads[a].wait()

        def pack(k, strips, a=a):
            cells = in_3d[a, k]
            if a < 2:
                return put_v(0, a * LEVELS + k, cells, strips)
            fx[MOVING + k, pl.ds(2, ROWS)] = cells
            return put_b(0, k, cells, strips)

        strips = lax.fori_loop(0, LEVELS, pack, strips, unroll=True)
    for a in range(3):
        loads[3 + a].wait()
    pl.semaphore_wait(barrier, total_near)
    sea, flow_u, flow_v = in_2d[0], in_2d[1], in_2d[2]
    send_state(0, strips, (sea, flow_u, flow_v, code))

    lane18 = lax.broadcasted_iota(jnp.int32, (ROWS + 2, LANES), 1)
    for step in range(STEPS):
        arrive(RIMS, step)
        if step:
            arrive(EARLY, step)
        from_left, from_right = y_recv[step, 1], y_recv[step, 4]
        near = jnp.where(odd, from_left, turn(from_right, -2, 1))
        far = jnp.where(odd, turn(from_left, 1, 1), turn(from_right, -3, 1))
        inner = turn(jnp.where(odd, strips[1], strips[0]), -1, 1)
        near_ext[pl.ds(1, ROWS)] = near
        odd8 = odd[0:8]
        top = jnp.where(odd8, y_recv[step, 0, 8:16], turn(y_recv[step, 3, 8:16], -2, 1))
        low = jnp.where(odd8, y_recv[step, 2, 0:8], turn(y_recv[step, 5, 0:8], -2, 1))
        near_ext[pl.ds(0, 1)] = top[7:8]
        near_ext[pl.ds(ROWS + 1, 1)] = low[0:1]

        if step == 0:
            code_ext[pl.ds(0, 1)] = x_recv[0, 0, pl.ds(CODE_ROW, 1)]
            code_ext[pl.ds(1, ROWS)] = code
            code_ext[pl.ds(ROWS + 1, 1)] = x_recv[0, 1, pl.ds(CODE_ROW, 1)]
            at = 2 * STACK
            code_near = jnp.where(
                odd,
                jnp.broadcast_to(near[:, at + 1 : at + 2], (ROWS, LANES)),
                jnp.broadcast_to(near[:, at : at + 1], (ROWS, LANES)),
            )
            act_near = ((pair & (LEVELS - 1)).astype(F32) < code_near).astype(F32)
            code18 = code_ext[pl.ds(0, ROWS + 2)]
        lap_near = act_near * (
            far + inner + near_ext[pl.ds(0, ROWS)] + near_ext[pl.ds(2, ROWS)] - 4.0 * near
        )
        near18 = near_ext[pl.ds(0, ROWS + 2)]

        def biharm(j, near_at, far_at, act18, keep):
            fx[j, pl.ds(0, 1)] = x_recv[step, 0, pl.ds(far_at, 1)]
            fx[j, pl.ds(1, 1)] = x_recv[step, 0, pl.ds(near_at, 1)]
            fx[j, pl.ds(ROWS + 2, 1)] = x_recv[step, 1, pl.ds(near_at, 1)]
            fx[j, pl.ds(ROWS + 3, 1)] = x_recv[step, 1, pl.ds(far_at, 1)]
            mid = fx[j, pl.ds(1, ROWS + 2)]
            edge = turn(near18, 127 - 2 * j, 1)
            ahead = jnp.where(lane18 == LANES - 1, edge, turn(mid, -1, 1))
            behind = jnp.where(lane18 == 0, edge, turn(mid, 1, 1))
            lap = act18 * (
                fx[j, pl.ds(0, ROWS + 2)] + fx[j, pl.ds(2, ROWS + 2)] + ahead + behind - 4.0 * mid
            )
            lp[j, pl.ds(0, ROWS + 2)] = lap
            if keep is not None:
                dyb[keep, pl.ds(0, ROWS + 2)] = ahead - behind
            mid = lp[j, pl.ds(1, ROWS)]
            edge = turn(lap_near, 127 - 2 * j, 1)
            ahead = jnp.where(lane == LANES - 1, edge, turn(mid, -1, 1))
            behind = jnp.where(lane == 0, edge, turn(mid, 1, 1))
            return lp[j, pl.ds(0, ROWS)] + lp[j, pl.ds(2, ROWS)] + ahead + behind - 4.0 * mid

        def level(k, carry):
            press_x, press_y, force_u, force_v, col_u, col_v = carry
            level_at = lax.convert_element_type(k, F32)
            act18 = (level_at < code18).astype(F32)
            act = (level_at < code).astype(F32)
            bih_u = biharm(k, k, MOVING + k, act18, None)
            bih_v = biharm(LEVELS + k, LEVELS + k, MOVING + LEVELS + k, act18, None)
            bih_b = biharm(
                MOVING + k, 2 * MOVING + k, 2 * MOVING + LEVELS + k, act18, k
            )
            u, v = fx[k, pl.ds(2, ROWS)], fx[LEVELS + k, pl.ds(2, ROWS)]
            at = 2 * LEVELS + k
            b = fx[at, pl.ds(2, ROWS)]
            b_x = fx[at, pl.ds(3, ROWS)] - fx[at, pl.ds(1, ROWS)]
            b_y = dyb[k, pl.ds(1, ROWS)]
            press_x, press_y = press_x + b_x, press_y + b_y
            tend_u = (-0.25 / LEVELS) * press_x + 0.1 * v - 0.02 * bih_u
            tend_v = (-0.25 / LEVELS) * press_y - 0.1 * u - 0.02 * bih_v
            tend_b = -0.5 * (u * b_x + v * b_y) - 0.02 * bih_b
            su = act * (u + 0.2 * tend_u)
            sv = act * (v + 0.2 * tend_v)
            star_u[k] = su
            star_v[k] = sv
            new_b = act * (b + 0.2 * tend_b)
            if step == STEPS - 1:
                out_b[k] = new_b
            else:
                fx[at, pl.ds(2, ROWS)] = new_b
            return (
                press_x, press_y, force_u + act * tend_u, force_v + act * tend_v,
                col_u + su, col_v + sv,
            )

        _, _, force_u, force_v, col_u, col_v = lax.fori_loop(
            0, LEVELS, level, (zero,) * 6, unroll=True
        )
        force_u, force_v = force_u / LEVELS, force_v / LEVELS
        fx_send[step, 0:ROWS] = force_u
        fx_send[step, ROWS : 2 * ROWS] = force_v
        flat_left, flat_right = pack_flat((force_u, force_v))
        fy_send[step, 0] = flat_left
        fy_send[step, 1] = flat_right
        start(FORCE, step)
        if step == STEPS - 1:
            out_columns[0] = col_u
            out_columns[1] = col_v
            stores = [
                pltpu.make_async_copy(src, dst, out_sem.at[i])
                for i, (src, dst) in enumerate((
                    (star_u, hbm_u), (star_v, hbm_v), (out_b, hbm_b), (out_columns, hbm_columns),
                    (out_wide.at[0:4], hbm_wide.at[0:4]), (out_wide.at[4:6], hbm_wide.at[4:6]),
                ))
            ]
            for store in stores[:4]:
                store.start()

        if step < STEPS - 1:
            def pack_b(k, strips):
                return put_b(step + 1, k, fx[MOVING + k, pl.ds(2, ROWS)], strips)

            strips = lax.fori_loop(0, LEVELS, pack_b, (zero, zero), unroll=True)
            start(EARLY, step + 1)
        arrive(PLANE, step)
        sides = [gy_recv[step, r] for r in range(6)]

        def plane(own, a):
            rows = slice(ROWS * a, ROWS * (a + 1))
            return wide(own, gx_recv[step, 0, rows], gx_recv[step, 1, rows], sides, a)

        if step == 0:
            code_wide = plane(code, 3)
        state = (plane(sea, 0), plane(flow_u, 1), plane(flow_v, 2))
        if step == STEPS - 1:
            for a, cells in enumerate(state + (code_wide,)):
                out_wide[a] = cells
            stores[4].start()
        arrive(FORCE, step)
        sides_f = [fy_recv[step, r] for r in range(6)]
        push_u, push_v = (
            0.2 * wide(
                own, fx_recv[step, 0, ROWS * a : ROWS * (a + 1)],
                fx_recv[step, 1, ROWS * a : ROWS * (a + 1)], sides_f, a,
            )
            for a, own in enumerate((force_u, force_v))
        )
        if step == STEPS - 1:
            out_wide[4] = push_u
            out_wide[5] = push_v
            stores[5].start()
        else:
            (sea, flow_u, flow_v), sum_u, sum_v = barotropic(state, push_u, push_v, code_wide)
            scale = LEVELS / SUB
            shift_u = (scale * sum_u - col_u) / lay
            shift_v = (scale * sum_v - col_v) / lay

            def couple(k, strips):
                act = (lax.convert_element_type(k, F32) < code).astype(F32)
                strips = put_v(step + 1, k, act * (star_u[k] + shift_u), strips)
                return put_v(step + 1, LEVELS + k, act * (star_v[k] + shift_v), strips)

            strips = lax.fori_loop(0, LEVELS, couple, strips, unroll=True)
            send_state(step + 1, strips, (sea, flow_u, flow_v))

    for step in range(STEPS):
        for phase in (RIMS, FORCE, PLANE, EARLY):
            if phase != EARLY or step:
                sent(phase, step)
    for store in stores:
        store.wait()


def per_device(velocity_u, velocity_v, buoyancy, surface, transport_u, transport_v, ocean, layers):
    cube = jax.ShapeDtypeStruct(velocity_u.shape, F32)
    flat = jax.ShapeDtypeStruct(surface.shape, F32)
    hbm = pl.BlockSpec(memory_space=pltpu.HBM)
    ext = 24
    columns = jax.ShapeDtypeStruct((2, ROWS, LANES), F32)
    planes = jax.ShapeDtypeStruct((6, 3 * ROWS, 2 * LANES), F32)
    block = (LEVELS, ROWS, LANES)
    middle = pl.pallas_call(
        kernel,
        out_shape=(cube, cube, cube, columns, planes),
        in_specs=[hbm] * 8,
        out_specs=(hbm,) * 5,
        scratch_shapes=[
            pltpu.VMEM(block, F32),
            pltpu.VMEM(block, F32),
            pltpu.VMEM(block, F32),
            pltpu.VMEM(columns.shape, F32),
            pltpu.VMEM(planes.shape, F32),
            pltpu.SemaphoreType.DMA((6,)),
            pltpu.VMEM((STACK, ext, LANES), F32),
            pltpu.VMEM((STACK, ext, LANES), F32),
            pltpu.VMEM((LEVELS, ext, LANES), F32),
            pltpu.VMEM((ext, LANES), F32),
            pltpu.VMEM((ext, LANES), F32),
            pltpu.VMEM((FIELDS,) + block, F32),
            pltpu.VMEM((3, ROWS, LANES), F32),
            pltpu.VMEM((2, ROWS, LANES), jnp.int32),
            pltpu.VMEM((STEPS, 2, RIM, LANES), F32),
            pltpu.VMEM((STEPS, 2, ROWS, LANES), F32),
            pltpu.VMEM((STEPS, 2, RIM, LANES), F32),
            pltpu.VMEM((STEPS, 6, ROWS, LANES), F32),
            pltpu.VMEM((STEPS, 4 * ROWS, LANES), F32),
            pltpu.VMEM((STEPS, 2, 8, LANES), F32),
            pltpu.VMEM((STEPS, 2, 4 * ROWS, LANES), F32),
            pltpu.VMEM((STEPS, 6, 8, LANES), F32),
            pltpu.VMEM((STEPS, 2 * ROWS, LANES), F32),
            pltpu.VMEM((STEPS, 2, 8, LANES), F32),
            pltpu.VMEM((STEPS, 2, 2 * ROWS, LANES), F32),
            pltpu.VMEM((STEPS, 6, 8, LANES), F32),
            pltpu.SemaphoreType.DMA((8,)),
            pltpu.SemaphoreType.DMA((4 * STEPS, 8)),
            pltpu.SemaphoreType.DMA((4 * STEPS, 8)),
        ],
        compiler_params=pltpu.CompilerParams(
            collective_id=0, has_side_effects=True, vmem_limit_bytes=60 * 2**20
        ),
    )(velocity_u, velocity_v, buoyancy, surface, transport_u, transport_v, ocean, layers)
    return tuple(
        pl.pallas_call(
            finish_kernel,
            out_shape=(cube, cube, cube, flat, flat, flat),
            in_specs=[hbm] * 5,
            out_specs=(hbm,) * 6,
            scratch_shapes=[
                pltpu.VMEM(block, F32),
                pltpu.VMEM(block, F32),
                pltpu.VMEM(columns.shape, F32),
                pltpu.VMEM(planes.shape, F32),
                pltpu.VMEM(block, F32),
                pltpu.VMEM(block, F32),
                pltpu.VMEM((3, ROWS, LANES), F32),
                pltpu.SemaphoreType.DMA((6,)),
                pltpu.SemaphoreType.DMA((4,)),
            ],
            compiler_params=pltpu.CompilerParams(vmem_limit_bytes=60 * 2**20),
        )(*middle)
    )


def solution(mesh):
    cube, flat = P(None, "gx", "gy"), P("gx", "gy")
    return jax.shard_map(
        per_device,
        mesh=mesh,
        in_specs=(cube, cube, cube, flat, flat, flat, flat, flat),
        out_specs=(cube, cube, cube, flat, flat, flat),
        check_vma=False,
    )
```

```python
import jax
import jax.numpy as jnp
from jax import lax
from jax.experimental import pallas as pl
from jax.experimental.pallas import tpu as pltpu
from jax.sharding import PartitionSpec as P

SUB = 8
STEPS = 2
LANES = 128
ROWS = 16
LEVELS = 16
FIELDS = 3
STACK = FIELDS * LEVELS
MESH = pl.DeviceIdType.MESH
F32 = jnp.float32

DIRS = [(-1, 0), (1, 0), (0, -1), (0, 1), (-1, -1), (-1, 1), (1, -1), (1, 1)]
SIDES = [(-1, -1), (0, -1), (1, -1), (-1, 1), (0, 1), (1, 1)]
MOVING = 2 * LEVELS
CODE_ROW = 2 * STACK
RIM = CODE_ROW + 8
HALF = LANES // 2


RIMS, FORCE, PLANE, EARLY = 0, 1, 2, 3


def turn(x, shift, axis):
    return pltpu.roll(x, shift % x.shape[axis] if isinstance(shift, int) else shift, axis)


def fold(cells):
    low = lax.broadcasted_iota(jnp.int32, (8, LANES), 1) < HALF
    return jnp.where(low, cells[0:8], turn(cells[8:16], HALF, 1))


def unfold(cells):
    return jnp.concatenate([cells, turn(cells, HALF, 1)], axis=0)


def pack_flat(arrays):
    lane = lax.broadcasted_iota(jnp.int32, (ROWS, LANES), 1)
    to_left = to_right = jnp.zeros((ROWS, LANES), F32)
    for a, cells in enumerate(arrays):
        to_right = jnp.where((lane >> 4) == a, turn(cells, 16 * a + 16, 1), to_right)
        to_left = jnp.where((lane >> 4) == a, turn(cells, 16 * a, 1), to_left)
    return fold(to_left), fold(to_right)


def wide(own, up, down, sides, a):
    lane = lax.broadcasted_iota(jnp.int32, (ROWS, LANES), 1)
    blocks = []
    for r in range(3):
        from_left, from_right = unfold(sides[r]), unfold(sides[r + 3])
        left, right = turn(from_left, 112 - 16 * a, 1), turn(from_right, -16 * a, 1)
        blocks.append(jnp.where(lane < 16, right, jnp.where(lane >= 112, left, 0.0)))
    main = jnp.concatenate([up, own, down], axis=0)
    return jnp.concatenate([main, jnp.concatenate(blocks, axis=0)], axis=1)


def barotropic(state, push_u, push_v, code_wide):
    wet = (code_wide > 0.0).astype(F32)
    depth = code_wide / LEVELS
    zero = jnp.zeros((ROWS, LANES), F32)

    def substep(_, carry):
        eta, tu, tv, sum_u, sum_v = carry
        div = (turn(tu, -1, 0) - turn(tu, 1, 0)) + (turn(tv, -1, 1) - turn(tv, 1, 1))
        eta = wet * (eta - 0.125 * div)
        thick = 0.125 * (depth + eta)
        new_u = wet * (
            0.98 * tu + push_u - thick * (turn(eta, -1, 0) - turn(eta, 1, 0)) + 0.05 * tv
        )
        new_v = wet * (
            0.98 * tv + push_v - thick * (turn(eta, -1, 1) - turn(eta, 1, 1)) - 0.05 * tu
        )
        sum_u = sum_u + new_u[ROWS : 2 * ROWS, 0:LANES]
        sum_v = sum_v + new_v[ROWS : 2 * ROWS, 0:LANES]
        return eta, new_u, new_v, sum_u, sum_v

    eta, tu, tv, sum_u, sum_v = lax.fori_loop(
        0, SUB, substep, state + (zero, zero), unroll=True
    )
    own = tuple(c[ROWS : 2 * ROWS, 0:LANES] for c in (eta, tu, tv))
    return own, sum_u, sum_v


def finish_kernel(
    hbm_u, hbm_v, new_b, hbm_columns, hbm_wide,
    out_u, out_v, out_b, out_eta, out_tu, out_tv,
    star_u, star_v, columns, wide_in, buf_u, buf_v, buf_flat, sem, in_sem,
):
    loads = [
        pltpu.make_async_copy(src, dst, in_sem.at[i])
        for i, (src, dst) in enumerate((
            (hbm_wide, wide_in), (hbm_columns, columns), (hbm_u, star_u), (hbm_v, star_v)
        ))
    ]
    for load in loads:
        load.start()
    copies = [pltpu.make_async_copy(new_b, out_b, sem.at[0])]
    copies[0].start()
    loads[0].wait()
    code_wide = wide_in[3]
    own, sum_u, sum_v = barotropic(
        (wide_in[0], wide_in[1], wide_in[2]), wide_in[4], wide_in[5], code_wide
    )
    for a, (cells, out) in enumerate(zip(own, (out_eta, out_tu, out_tv))):
        buf_flat[a] = cells
        copies.append(pltpu.make_async_copy(buf_flat.at[a], out, sem.at[1 + a]))
        copies[-1].start()
    code = code_wide[ROWS : 2 * ROWS, 0:LANES]
    lay = jnp.maximum(code, 1.0)
    scale = LEVELS / SUB
    for load in loads[1:]:
        load.wait()
    for a, (star, buf, out, total) in enumerate(
        ((star_u, buf_u, out_u, sum_u), (star_v, buf_v, out_v, sum_v))
    ):
        shift = (scale * total - columns[a]) / lay

        def finish(k, carry, star=star, buf=buf, shift=shift):
            act = lax.convert_element_type(k, F32) < code
            buf[k] = jnp.where(act, star[k] + shift, 0.0)
            return carry

        lax.fori_loop(0, LEVELS, finish, 0, unroll=True)
        copies.append(pltpu.make_async_copy(buf, out, sem.at[4 + a]))
        copies[-1].start()
    for copy in copies:
        copy.wait()


def kernel(
    vel_u, vel_v, buoy, surface, trans_u, trans_v, ocean, layers,
    hbm_u, hbm_v, hbm_b, hbm_columns, hbm_wide,
    star_u, star_v, out_b, out_columns, out_wide, out_sem,
    fx, lp, dyb, near_ext, code_ext, in_3d, in_2d, in_int,
    x_send, y_send, x_recv, y_recv, gx_send, gy_send, gx_recv, gy_recv,
    fx_send, fy_send, fx_recv, fy_recv, in_sem, send_sem, recv_sem,
):
    loads = []
    for a, ref in enumerate((vel_u, vel_v, buoy)):
        loads.append(pltpu.make_async_copy(ref, in_3d.at[a], in_sem.at[a]))
    for a, ref in enumerate((surface, trans_u, trans_v)):
        loads.append(pltpu.make_async_copy(ref, in_2d.at[a], in_sem.at[3 + a]))
    for a, ref in enumerate((ocean, layers)):
        loads.append(pltpu.make_async_copy(ref, in_int.at[a], in_sem.at[6 + a]))
    for load in loads:
        load.start()
    gx, gy = lax.axis_index("gx"), lax.axis_index("gy")
    nx, ny = lax.axis_size("gx"), lax.axis_size("gy")

    def exists(d):
        ok = jnp.bool_(True)
        if d[0] == -1:
            ok = jnp.logical_and(ok, gx > 0)
        if d[0] == 1:
            ok = jnp.logical_and(ok, gx < nx - 1)
        if d[1] == -1:
            ok = jnp.logical_and(ok, gy > 0)
        if d[1] == 1:
            ok = jnp.logical_and(ok, gy < ny - 1)
        return ok

    here = {d: exists(d) for d in DIRS}
    barrier = pltpu.get_barrier_semaphore()
    total_near = jnp.int32(0)
    for d in DIRS:
        total_near = total_near + here[d].astype(jnp.int32)

        @pl.when(here[d])
        def _(d=d):
            pl.semaphore_signal(barrier, inc=1, device_id=(gx + d[0], gy + d[1]), device_id_type=MESH)

    for d in DIRS:
        @pl.when(jnp.logical_not(here[d]))
        def _(d=d):
            for p in range(STEPS):
                if d[1] == 0:
                    s = 0 if d[0] < 0 else 1
                    x_recv[p, s] = jnp.zeros(x_recv.shape[2:], F32)
                    gx_recv[p, s] = jnp.zeros(gx_recv.shape[2:], F32)
                    fx_recv[p, s] = jnp.zeros(fx_recv.shape[2:], F32)
                else:
                    s = SIDES.index(d)
                    y_recv[p, s] = jnp.zeros(y_recv.shape[2:], F32)
                    gy_recv[p, s] = jnp.zeros(gy_recv.shape[2:], F32)
                    fy_recv[p, s] = jnp.zeros(fy_recv.shape[2:], F32)

    def copies(phase, step):
        result = []
        for i, d in enumerate(DIRS):
            back = (-d[0], -d[1])
            if d[1] == 0:
                src_at, dst_at = (0 if d[0] < 0 else 1), (0 if back[0] < 0 else 1)
                if phase == FORCE:
                    src, dst = fx_send.at[step], fx_recv.at[step, dst_at]
                elif phase == PLANE:
                    rows = pl.ds(0, (4 if step == 0 else 3) * ROWS)
                    src, dst = gx_send.at[step, rows], gx_recv.at[step, dst_at, rows]
                else:
                    if step == 0:
                        rows = pl.ds(0, RIM)
                    elif phase == EARLY:
                        rows = pl.ds(2 * MOVING, 2 * LEVELS)
                    else:
                        rows = pl.ds(0, 2 * MOVING)
                    src, dst = x_send.at[step, src_at, rows], x_recv.at[step, dst_at, rows]
            else:
                src_at, dst_at = (0 if d[1] < 0 else 1), SIDES.index(back)
                if phase == FORCE:
                    src, dst = fy_send.at[step, src_at], fy_recv.at[step, dst_at]
                elif phase == PLANE:
                    src, dst = gy_send.at[step, src_at], gy_recv.at[step, dst_at]
                elif phase == EARLY:
                    continue
                else:
                    src, dst = y_send.at[step, src_at], y_recv.at[step, dst_at]
                    if d[0] != 0:
                        rows = pl.ds(0, 8) if d[0] < 0 else pl.ds(8, 8)
                        src, dst = src.at[rows], dst.at[rows]
            at = phase * STEPS + step
            copy = pltpu.make_async_remote_copy(
                src_ref=src, dst_ref=dst,
                send_sem=send_sem.at[at, i], recv_sem=recv_sem.at[at, DIRS.index(back)],
                device_id=(gx + d[0], gy + d[1]), device_id_type=MESH,
            )
            result.append((d, copy))
        return result

    def start(phase, step):
        for d, copy in copies(phase, step):
            @pl.when(here[d])
            def _(copy=copy):
                copy.start()

    def arrive(phase, step):
        by_dir = dict(copies(phase, step))
        for d in by_dir:
            @pl.when(here[d])
            def _(d=d):
                by_dir[(-d[0], -d[1])].wait_recv()

    def sent(phase, step):
        for d, copy in copies(phase, step):
            @pl.when(here[d])
            def _(copy=copy):
                copy.wait_send()

    lane = lax.broadcasted_iota(jnp.int32, (ROWS, LANES), 1)
    pair = lane >> 1
    odd = (lane & 1) == 1
    zero = jnp.zeros((ROWS, LANES), F32)

    def put(step, j, near_at, far_at, cells, strips):
        x_send[step, 0, pl.ds(near_at, 1)] = cells[0:1]
        x_send[step, 0, pl.ds(far_at, 1)] = cells[1:2]
        x_send[step, 1, pl.ds(near_at, 1)] = cells[ROWS - 1 : ROWS]
        x_send[step, 1, pl.ds(far_at, 1)] = cells[ROWS - 2 : ROWS - 1]
        to_left, to_right = strips
        rolled = turn(cells, 2 * j + 2, 1)
        to_right = jnp.where(pair == j, rolled, to_right)
        to_left = jnp.where(pair == j + 1, rolled, to_left)
        return to_left, to_right

    def put_v(step, j, cells, strips):
        fx[j, pl.ds(2, ROWS)] = cells
        return put(step, j, j, MOVING + j, cells, strips)

    def put_b(step, k, cells, strips):
        j = MOVING + k
        return put(step, j, 2 * MOVING + k, 2 * MOVING + LEVELS + k, cells, strips)

    def send_state(step, strips, flats):
        y_send[step, 0] = strips[0]
        y_send[step, 1] = strips[1]
        start(RIMS, step)
        flat_left, flat_right = pack_flat(flats)
        gy_send[step, 0] = flat_left
        gy_send[step, 1] = flat_right
        for a, cells in enumerate(flats):
            gx_send[step, ROWS * a : ROWS * (a + 1)] = cells
        start(PLANE, step)

    loads[6].wait()
    loads[7].wait()
    lay = in_int[1].astype(F32)
    code = jnp.where(in_int[0] > 0, lay, 0.0)
    strips = put(0, STACK, CODE_ROW, CODE_ROW + 1, code, (zero, zero))
    for a in range(FIELDS):
        loads[a].wait()

        def pack(k, strips, a=a):
            cells = in_3d[a, k]
            if a < 2:
                return put_v(0, a * LEVELS + k, cells, strips)
            fx[MOVING + k, pl.ds(2, ROWS)] = cells
            return put_b(0, k, cells, strips)

        strips = lax.fori_loop(0, LEVELS, pack, strips, unroll=True)
    for a in range(3):
        loads[3 + a].wait()
    pl.semaphore_wait(barrier, total_near)
    sea, flow_u, flow_v = in_2d[0], in_2d[1], in_2d[2]
    send_state(0, strips, (sea, flow_u, flow_v, code))

    lane18 = lax.broadcasted_iota(jnp.int32, (ROWS + 2, LANES), 1)
    for step in range(STEPS):
        arrive(RIMS, step)
        if step:
            arrive(EARLY, step)
        from_left, from_right = y_recv[step, 1], y_recv[step, 4]
        near = jnp.where(odd, from_left, turn(from_right, -2, 1))
        far = jnp.where(odd, turn(from_left, 1, 1), turn(from_right, -3, 1))
        inner = turn(jnp.where(odd, strips[1], strips[0]), -1, 1)
        near_ext[pl.ds(1, ROWS)] = near
        odd8 = odd[0:8]
        top = jnp.where(odd8, y_recv[step, 0, 8:16], turn(y_recv[step, 3, 8:16], -2, 1))
        low = jnp.where(odd8, y_recv[step, 2, 0:8], turn(y_recv[step, 5, 0:8], -2, 1))
        near_ext[pl.ds(0, 1)] = top[7:8]
        near_ext[pl.ds(ROWS + 1, 1)] = low[0:1]

        if step == 0:
            code_ext[pl.ds(0, 1)] = x_recv[0, 0, pl.ds(CODE_ROW, 1)]
            code_ext[pl.ds(1, ROWS)] = code
            code_ext[pl.ds(ROWS + 1, 1)] = x_recv[0, 1, pl.ds(CODE_ROW, 1)]
            at = 2 * STACK
            code_near = jnp.where(
                odd,
                jnp.broadcast_to(near[:, at + 1 : at + 2], (ROWS, LANES)),
                jnp.broadcast_to(near[:, at : at + 1], (ROWS, LANES)),
            )
            act_near = ((pair & (LEVELS - 1)).astype(F32) < code_near).astype(F32)
            code18 = code_ext[pl.ds(0, ROWS + 2)]
        lap_near = act_near * (
            far + inner + near_ext[pl.ds(0, ROWS)] + near_ext[pl.ds(2, ROWS)] - 4.0 * near
        )
        near18 = near_ext[pl.ds(0, ROWS + 2)]

        def biharm(j, near_at, far_at, act18):
            fx[j, pl.ds(0, 1)] = x_recv[step, 0, pl.ds(far_at, 1)]
            fx[j, pl.ds(1, 1)] = x_recv[step, 0, pl.ds(near_at, 1)]
            fx[j, pl.ds(ROWS + 2, 1)] = x_recv[step, 1, pl.ds(near_at, 1)]
            fx[j, pl.ds(ROWS + 3, 1)] = x_recv[step, 1, pl.ds(far_at, 1)]
            mid = fx[j, pl.ds(1, ROWS + 2)]
            edge = turn(near18, 127 - 2 * j, 1)
            ahead = jnp.where(lane18 == LANES - 1, edge, turn(mid, -1, 1))
            behind = jnp.where(lane18 == 0, edge, turn(mid, 1, 1))
            lap = act18 * (
                fx[j, pl.ds(0, ROWS + 2)] + fx[j, pl.ds(2, ROWS + 2)] + ahead + behind - 4.0 * mid
            )
            lp[j, pl.ds(0, ROWS + 2)] = lap
            mid = lp[j, pl.ds(1, ROWS)]
            edge = turn(lap_near, 127 - 2 * j, 1)
            ahead = jnp.where(lane == LANES - 1, edge, turn(mid, -1, 1))
            behind = jnp.where(lane == 0, edge, turn(mid, 1, 1))
            return lp[j, pl.ds(0, ROWS)] + lp[j, pl.ds(2, ROWS)] + ahead + behind - 4.0 * mid

        def buoyancy(k, carry):
            level_at = lax.convert_element_type(k, F32)
            act18 = (level_at < code18).astype(F32)
            act = (level_at < code).astype(F32)
            at = 2 * LEVELS + k
            bih_b = biharm(at, 2 * MOVING + k, 2 * MOVING + LEVELS + k, act18)
            u, v = fx[k, pl.ds(2, ROWS)], fx[LEVELS + k, pl.ds(2, ROWS)]
            b = fx[at, pl.ds(2, ROWS)]
            b_x = fx[at, pl.ds(3, ROWS)] - fx[at, pl.ds(1, ROWS)]
            tend_b = -0.5 * (u * b_x + v * dyb[k, pl.ds(0, ROWS)]) - 0.02 * bih_b
            new_b = act * (b + 0.2 * tend_b)
            if step == STEPS - 1:
                out_b[k] = new_b
            else:
                fx[at, pl.ds(2, ROWS)] = new_b
            return carry

        def level(k, carry):
            press_x, press_y, force_u, force_v, col_u, col_v = carry
            level_at = lax.convert_element_type(k, F32)
            act18 = (level_at < code18).astype(F32)
            act = (level_at < code).astype(F32)
            bih_u = biharm(k, k, MOVING + k, act18)
            bih_v = biharm(LEVELS + k, LEVELS + k, MOVING + LEVELS + k, act18)
            u, v = fx[k, pl.ds(2, ROWS)], fx[LEVELS + k, pl.ds(2, ROWS)]
            at = 2 * LEVELS + k
            fx[at, pl.ds(1, 1)] = x_recv[step, 0, pl.ds(2 * MOVING + k, 1)]
            fx[at, pl.ds(ROWS + 2, 1)] = x_recv[step, 1, pl.ds(2 * MOVING + k, 1)]
            b = fx[at, pl.ds(2, ROWS)]
            edge = turn(near, 127 - 2 * at, 1)
            b_x = fx[at, pl.ds(3, ROWS)] - fx[at, pl.ds(1, ROWS)]
            b_y = jnp.where(lane == LANES - 1, edge, turn(b, -1, 1)) - jnp.where(
                lane == 0, edge, turn(b, 1, 1)
            )
            dyb[k, pl.ds(0, ROWS)] = b_y
            press_x, press_y = press_x + b_x, press_y + b_y
            tend_u = (-0.25 / LEVELS) * press_x + 0.1 * v - 0.02 * bih_u
            tend_v = (-0.25 / LEVELS) * press_y - 0.1 * u - 0.02 * bih_v
            su = act * (u + 0.2 * tend_u)
            sv = act * (v + 0.2 * tend_v)
            star_u[k] = su
            star_v[k] = sv
            return (
                press_x, press_y, force_u + act * tend_u, force_v + act * tend_v,
                col_u + su, col_v + sv,
            )

        _, _, force_u, force_v, col_u, col_v = lax.fori_loop(
            0, LEVELS, level, (zero,) * 6, unroll=True
        )
        force_u, force_v = force_u / LEVELS, force_v / LEVELS
        fx_send[step, 0:ROWS] = force_u
        fx_send[step, ROWS : 2 * ROWS] = force_v
        flat_left, flat_right = pack_flat((force_u, force_v))
        fy_send[step, 0] = flat_left
        fy_send[step, 1] = flat_right
        start(FORCE, step)
        lax.fori_loop(0, LEVELS, buoyancy, 0, unroll=True)
        if step == STEPS - 1:
            out_columns[0] = col_u
            out_columns[1] = col_v
            stores = [
                pltpu.make_async_copy(src, dst, out_sem.at[i])
                for i, (src, dst) in enumerate((
                    (star_u, hbm_u), (star_v, hbm_v), (out_b, hbm_b), (out_columns, hbm_columns),
                    (out_wide.at[0:4], hbm_wide.at[0:4]), (out_wide.at[4:6], hbm_wide.at[4:6]),
                ))
            ]
            for store in stores[:4]:
                store.start()

        if step < STEPS - 1:
            def pack_b(k, strips):
                return put_b(step + 1, k, fx[MOVING + k, pl.ds(2, ROWS)], strips)

            strips = lax.fori_loop(0, LEVELS, pack_b, (zero, zero), unroll=True)
            start(EARLY, step + 1)
        arrive(PLANE, step)
        sides = [gy_recv[step, r] for r in range(6)]

        def plane(own, a):
            rows = slice(ROWS * a, ROWS * (a + 1))
            return wide(own, gx_recv[step, 0, rows], gx_recv[step, 1, rows], sides, a)

        if step == 0:
            code_wide = plane(code, 3)
        state = (plane(sea, 0), plane(flow_u, 1), plane(flow_v, 2))
        if step == STEPS - 1:
            for a, cells in enumerate(state + (code_wide,)):
                out_wide[a] = cells
            stores[4].start()
        arrive(FORCE, step)
        sides_f = [fy_recv[step, r] for r in range(6)]
        push_u, push_v = (
            0.2 * wide(
                own, fx_recv[step, 0, ROWS * a : ROWS * (a + 1)],
                fx_recv[step, 1, ROWS * a : ROWS * (a + 1)], sides_f, a,
            )
            for a, own in enumerate((force_u, force_v))
        )
        if step == STEPS - 1:
            out_wide[4] = push_u
            out_wide[5] = push_v
            stores[5].start()
        else:
            (sea, flow_u, flow_v), sum_u, sum_v = barotropic(state, push_u, push_v, code_wide)
            scale = LEVELS / SUB
            shift_u = (scale * sum_u - col_u) / lay
            shift_v = (scale * sum_v - col_v) / lay

            def couple(k, strips):
                act = (lax.convert_element_type(k, F32) < code).astype(F32)
                strips = put_v(step + 1, k, act * (star_u[k] + shift_u), strips)
                return put_v(step + 1, LEVELS + k, act * (star_v[k] + shift_v), strips)

            strips = lax.fori_loop(0, LEVELS, couple, strips, unroll=True)
            send_state(step + 1, strips, (sea, flow_u, flow_v))

    for step in range(STEPS):
        for phase in (RIMS, FORCE, PLANE, EARLY):
            if phase != EARLY or step:
                sent(phase, step)
    for store in stores:
        store.wait()


def per_device(velocity_u, velocity_v, buoyancy, surface, transport_u, transport_v, ocean, layers):
    cube = jax.ShapeDtypeStruct(velocity_u.shape, F32)
    flat = jax.ShapeDtypeStruct(surface.shape, F32)
    hbm = pl.BlockSpec(memory_space=pltpu.HBM)
    ext = 24
    columns = jax.ShapeDtypeStruct((2, ROWS, LANES), F32)
    planes = jax.ShapeDtypeStruct((6, 3 * ROWS, 2 * LANES), F32)
    block = (LEVELS, ROWS, LANES)
    middle = pl.pallas_call(
        kernel,
        out_shape=(cube, cube, cube, columns, planes),
        in_specs=[hbm] * 8,
        out_specs=(hbm,) * 5,
        scratch_shapes=[
            pltpu.VMEM(block, F32),
            pltpu.VMEM(block, F32),
            pltpu.VMEM(block, F32),
            pltpu.VMEM(columns.shape, F32),
            pltpu.VMEM(planes.shape, F32),
            pltpu.SemaphoreType.DMA((6,)),
            pltpu.VMEM((STACK, ext, LANES), F32),
            pltpu.VMEM((STACK, ext, LANES), F32),
            pltpu.VMEM((LEVELS, ext, LANES), F32),
            pltpu.VMEM((ext, LANES), F32),
            pltpu.VMEM((ext, LANES), F32),
            pltpu.VMEM((FIELDS,) + block, F32),
            pltpu.VMEM((3, ROWS, LANES), F32),
            pltpu.VMEM((2, ROWS, LANES), jnp.int32),
            pltpu.VMEM((STEPS, 2, RIM, LANES), F32),
            pltpu.VMEM((STEPS, 2, ROWS, LANES), F32),
            pltpu.VMEM((STEPS, 2, RIM, LANES), F32),
            pltpu.VMEM((STEPS, 6, ROWS, LANES), F32),
            pltpu.VMEM((STEPS, 4 * ROWS, LANES), F32),
            pltpu.VMEM((STEPS, 2, 8, LANES), F32),
            pltpu.VMEM((STEPS, 2, 4 * ROWS, LANES), F32),
            pltpu.VMEM((STEPS, 6, 8, LANES), F32),
            pltpu.VMEM((STEPS, 2 * ROWS, LANES), F32),
            pltpu.VMEM((STEPS, 2, 8, LANES), F32),
            pltpu.VMEM((STEPS, 2, 2 * ROWS, LANES), F32),
            pltpu.VMEM((STEPS, 6, 8, LANES), F32),
            pltpu.SemaphoreType.DMA((8,)),
            pltpu.SemaphoreType.DMA((4 * STEPS, 8)),
            pltpu.SemaphoreType.DMA((4 * STEPS, 8)),
        ],
        compiler_params=pltpu.CompilerParams(
            collective_id=0, has_side_effects=True, vmem_limit_bytes=60 * 2**20
        ),
    )(velocity_u, velocity_v, buoyancy, surface, transport_u, transport_v, ocean, layers)
    return tuple(
        pl.pallas_call(
            finish_kernel,
            out_shape=(cube, cube, cube, flat, flat, flat),
            in_specs=[hbm] * 5,
            out_specs=(hbm,) * 6,
            scratch_shapes=[
                pltpu.VMEM(block, F32),
                pltpu.VMEM(block, F32),
                pltpu.VMEM(columns.shape, F32),
                pltpu.VMEM(planes.shape, F32),
                pltpu.VMEM(block, F32),
                pltpu.VMEM(block, F32),
                pltpu.VMEM((3, ROWS, LANES), F32),
                pltpu.SemaphoreType.DMA((6,)),
                pltpu.SemaphoreType.DMA((4,)),
            ],
            compiler_params=pltpu.CompilerParams(vmem_limit_bytes=60 * 2**20),
        )(*middle)
    )


def solution(mesh):
    cube, flat = P(None, "gx", "gy"), P("gx", "gy")
    return jax.shard_map(
        per_device,
        mesh=mesh,
        in_specs=(cube, cube, cube, flat, flat, flat, flat, flat),
        out_specs=(cube, cube, cube, flat, flat, flat),
        check_vma=False,
    )
```
